32 devices in a mesh: row: 8 (over y, x, core), col: 4 (over z).
Axes of the slice: x: 2, y: 2, z: 4, core: 2. Of those that a mesh axis runs over, the one named last changes fastest.
Arguments:
- covariance: bfloat16 [2048, 2048], P('row', 'col'), may hold values from -16 to 16
- reflectors: bfloat16 [2048, 128], P('row'), may hold values from -0.5 to 0.5
- factor: float32 [128, 128], replicated, may hold values from -0.5 to 2, as said below
Outputs:
- updated: float32 [2048, 2048], P('row', 'col')
The draws below stay inside these ranges and needn't reach their ends.
Inputs may be any that keep to these rules, and one draw needn't show every extreme that they name: factor is upper triangular with a diagonal of 1 to 2.
All inputs are finite; a program needn't handle non-finite values.
Results may differ from the reference program's by a relative error of at most 0.0003.
Values may be sent and summed in bfloat16 or wider, within the bound.
No kernel may reach another device: no remote copies, remote signals or barrier semaphores. Data moves between devices by JAX's collectives and lax.ppermute only.
A program may use at most 64 MiB of HBM per device.

```python
import jax
import jax.numpy as jnp
from jax import lax

BAND = 128
ORDER = 2048


def draw_covariance(key, part):
    first = jax.random.fold_in(key, 0)
    normal = jax.random.normal(first, (ORDER, ORDER), jnp.float32)
    matrix = (normal + normal.T) * 0.7071
    return jnp.clip(matrix, -16.0, 16.0).astype(jnp.bfloat16)


def draw_factor(key, part):
    first, second = jax.random.split(key)
    diag_part = jax.random.uniform(first, (BAND,), jnp.float32, 1.0, 2.0)
    upper = jnp.clip(jax.random.normal(second, (BAND, BAND), jnp.float32) * BAND ** (-0.5), -0.5, 0.5)
    return jnp.triu(upper, 1) + jnp.diag(diag_part)


def steps_of(key, dims, shards, least, top_value):
    gain, own = 1.0, jax.random.fold_in(key, 6)
    for dim, shards_of in shards:
        steps = jnp.exp(jax.random.uniform(jax.random.fold_in(own, dim), (shards_of,), jnp.float32, least / len(shards), top_value / len(shards)))
        gain = gain * jnp.repeat(steps, dims[dim] // shards_of).reshape([-1 if axis == dim else 1 for axis in range(len(dims))])
    return gain


def scatter_about(rng, shape, deviation, bound, cuts=(), held_as=jnp.bfloat16):
    result = jax.random.normal(rng, shape, jnp.float32) * deviation
    if len(cuts) > 0:
        result = steps_of(rng, shape, cuts, -0.22, 0.18) * result
    return jnp.clip(result, min=-bound, max=bound).astype(held_as)


def setup_inputs(seed: int = 0) -> dict:
    keys = jax.random.split(jax.random.key(seed), 4)
    covariance = draw_covariance(jax.random.fold_in(keys[3], 71), 0)
    reflectors = scatter_about(keys[1], (ORDER, BAND), (ORDER // 16) ** -0.5, 0.5, ((0, 8),))
    factor = draw_factor(jax.random.fold_in(keys[3], 71), 0)
    return {"covariance": covariance, "reflectors": reflectors, "factor": factor}


def reference(covariance, reflectors, factor):
    highest = lax.Precision.HIGHEST
    panel = jnp.dot(covariance, reflectors, preferred_element_type=jnp.float32)
    mixed = jnp.dot(panel, factor, precision=highest)
    vectors = reflectors.astype(jnp.float32)
    gram = jnp.dot(vectors.T, mixed, precision=highest)
    correction = jnp.dot(factor.T, gram, precision=highest)
    update_cols = mixed - 0.5 * jnp.dot(vectors, correction, precision=highest)
    updated = covariance.astype(jnp.float32) - jnp.dot(vectors, update_cols.T, precision=highest)
    return updated - jnp.dot(update_cols, vectors.T, precision=highest)
```

```python
import jax
import jax.numpy as jnp
from jax import lax
from jax.sharding import PartitionSpec as P


def solution(mesh):
    n_row, n_col = mesh.shape["row"], mesh.shape["col"]
    q = n_row // n_col
    highest = lax.Precision.HIGHEST

    def device(k, h, c):
        return (k * q + h) * n_col + c

    mirror = [
        (device(c, h, k), device(k, h, c))
        for k in range(n_col) for h in range(q) for c in range(n_col)
    ]

    def member(x, s):
        return lax.ppermute(x, "row", [(r, r ^ s) for r in range(n_row)])

    def group(x, s):
        return lax.ppermute(x, "row", [(r, r ^ (s * q)) for r in range(n_row)])

    def plane(x, s):
        return lax.ppermute(x, "col", [(c, c ^ s) for c in range(n_col)])

    def from_mirror(x):
        return lax.ppermute(x, ("row", "col"), mirror)

    def dot(a, b, dims):
        return lax.dot_general(a, b, (dims, ((), ())), precision=highest, preferred_element_type=jnp.float32)

    def gathered(own, pieces, h):
        rows = own.shape[0]
        whole = jnp.zeros((q * rows, own.shape[1]), own.dtype)
        for s, piece in enumerate([own] + pieces):
            whole = lax.dynamic_update_slice_in_dim(whole, piece, (h ^ s) * rows, 0)
        return whole

    def shards(covariance, reflectors, factor):
        rows = covariance.shape[0]
        h = lax.rem(lax.axis_index("row"), q)
        back = lax.dot_general(
            covariance, reflectors, (((0,), (0,)), ((), ())), preferred_element_type=jnp.float32
        )
        piece = lax.dynamic_slice_in_dim(back, h * rows, rows, 0)
        for s in range(1, q):
            piece = piece + member(lax.dynamic_slice_in_dim(back, (h ^ s) * rows, rows, 0), s)
        total = piece
        for s in range(1, n_col):
            total = total + group(piece, s)
        v_piece = from_mirror(reflectors)
        v_cols = gathered(v_piece, [member(v_piece, s) for s in range(1, q)], h)
        p_cols = gathered(total, [member(total, s) for s in range(1, q)], h)
        p_rows = from_mirror(total)
        gram = dot(v_piece.astype(jnp.float32), total, ((0,), (0,)))
        summed = gram
        for s in range(1, n_col):
            summed = summed + plane(gram, s)
        whole = summed
        for s in range(1, q):
            whole = whole + member(summed, s)
        y_rows = dot(reflectors.astype(jnp.float32), factor, ((1,), (1,)))
        y_cols = dot(v_cols.astype(jnp.float32), factor, ((1,), (1,)))
        first = covariance.astype(jnp.float32) - dot(y_rows, p_cols, ((1,), (1,)))
        x_rows = p_rows - dot(y_rows, whole, ((1,), (0,)))
        return first - dot(x_rows, y_cols, ((1,), (1,)))

    in_specs = (P("row", "col"), P("row", None), P())
    return jax.shard_map(shards, mesh=mesh, in_specs=in_specs, out_specs=P("row", "col"), check_vma=False)
```

```python
import jax
import jax.numpy as jnp
from jax import lax
from jax.sharding import PartitionSpec as P

TOP = 30719.0
LEAST = -100.0
TILE = 16


def scale_of(ratio, exponent):
    return ratio.astype(jnp.float32) * jnp.exp2(exponent.astype(jnp.float32))


def encode(x):
    top = jnp.max(jnp.abs(x), axis=0, keepdims=True)
    exponent = jnp.maximum(jnp.ceil(jnp.log2(top)), LEAST).astype(jnp.float16)
    ratio = jnp.minimum(top * jnp.exp2(-exponent.astype(jnp.float32)) * 1.001, 2.0).astype(jnp.float16)
    ratio = jnp.maximum(ratio, jnp.float16(0.25))
    step = TOP / scale_of(ratio, exponent)
    code = jnp.minimum(jnp.abs(x) * step + 0.5, TOP).astype(jnp.int32)
    power = lax.shift_left(jnp.int32(1), lax.shift_right_logical(code, 10)).astype(jnp.float32)
    size = (jnp.bitwise_and(code, 1023) + 1024).astype(jnp.float32) * power * 2.0**-24
    coded = jnp.where(x < 0, -size, size).astype(jnp.float16)
    width = x.shape[1]
    tail = jnp.concatenate(
        [jnp.broadcast_to(ratio, (TILE // 2, width)), jnp.broadcast_to(exponent, (TILE // 2, width))], 0
    )
    return jnp.concatenate([coded, tail], 0)


def decode(message):
    rows = message.shape[0] - TILE
    y = message[:rows].astype(jnp.float32)
    size = jnp.abs(y) * 2.0**14
    order = 31 - lax.clz(size.astype(jnp.int32))
    inverse = lax.shift_left(jnp.int32(1), 30 - order).astype(jnp.float32) * 2.0**-30
    code = 1024.0 * (order.astype(jnp.float32) + (size * inverse - 1.0))
    step = scale_of(message[rows : rows + 1], message[rows + TILE // 2 : rows + TILE // 2 + 1]) * (1.0 / TOP)
    return jnp.where(y < 0, -code, code) * step


def solution(mesh):
    n_row, n_col = mesh.shape["row"], mesh.shape["col"]
    q = n_row // n_col
    highest = lax.Precision.HIGHEST

    def member(x, s):
        return lax.ppermute(x, "row", [(r, r ^ s) for r in range(n_row)])

    def group(x, s):
        return lax.ppermute(x, "row", [(r, r ^ (s * q)) for r in range(n_row)])

    def plane(x, s):
        return lax.ppermute(x, "col", [(c, c ^ s) for c in range(n_col)])

    def dot(a, b, dims):
        return lax.dot_general(a, b, (dims, ((), ())), precision=highest, preferred_element_type=jnp.float32)

    def placed(pieces, me):
        rows = pieces[0].shape[0]
        whole = jnp.zeros((len(pieces) * rows, pieces[0].shape[1]), pieces[0].dtype)
        for s, piece in enumerate(pieces):
            whole = lax.dynamic_update_slice_in_dim(whole, piece, (me ^ s) * rows, 0)
        return whole

    def shards(covariance, reflectors, factor):
        rows = covariance.shape[0]
        row, c = lax.axis_index("row"), lax.axis_index("col")
        k, h = lax.div(row, q), lax.rem(row, q)
        back = lax.dot_general(
            covariance, reflectors, (((0,), (0,)), ((), ())), preferred_element_type=jnp.float32
        )
        piece = lax.dynamic_slice_in_dim(back, h * rows, rows, 0)
        for s in range(1, q):
            piece = piece + member(lax.dynamic_slice_in_dim(back, (h ^ s) * rows, rows, 0), s)
        message = encode(piece)
        others = [group(message, s) for s in range(1, n_col)]
        held, _ = lax.optimization_barrier((reflectors, message))
        v_mates = placed([held] + [group(held, s) for s in range(1, n_col)], k)
        total = piece
        for other in others:
            total = total + decode(other)
        message = encode(total)
        p_mates = placed([total] + [decode(plane(message, s)) for s in range(1, n_col)], c)
        p_cols = placed([total] + [member(total, s) for s in range(1, q)], h)
        v_piece = lax.dynamic_slice_in_dim(v_mates, c * rows, rows, 0)
        v_cols = placed([v_piece] + [member(v_piece, s) for s in range(1, q)], h)
        gram = dot(v_mates.astype(jnp.float32), p_mates, ((0,), (0,)))
        whole = gram
        for s in range(1, q):
            whole = whole + member(gram, s)
        p_rows = lax.dynamic_slice_in_dim(p_mates, k * rows, rows, 0)
        y_rows = dot(reflectors.astype(jnp.float32), factor, ((1,), (1,)))
        y_cols = dot(v_cols.astype(jnp.float32), factor, ((1,), (1,)))
        first = covariance.astype(jnp.float32) - dot(y_rows, p_cols, ((1,), (1,)))
        x_rows = p_rows - dot(y_rows, whole, ((1,), (0,)))
        return first - dot(x_rows, y_cols, ((1,), (1,)))

    in_specs = (P("row", "col"), P("row", None), P())
    return jax.shard_map(shards, mesh=mesh, in_specs=in_specs, out_specs=P("row", "col"), check_vma=False)
```

```python
import jax
import jax.numpy as jnp
from jax import lax
from jax.sharding import PartitionSpec as P

TOP = 30719.0
LEAST = -100.0
TILE = 16


def scale_of(ratio, exponent):
    return ratio.astype(jnp.float32) * jnp.exp2(exponent.astype(jnp.float32))


def encode(x):
    top = jnp.max(jnp.abs(x), axis=0, keepdims=True)
    exponent = lax.reduce_precision(jnp.maximum(jnp.ceil(jnp.log2(top)), LEAST), 5, 10).astype(jnp.float16)
    ratio = jnp.clip(top * jnp.exp2(-exponent.astype(jnp.float32)) * 1.001, 0.25, 2.0)
    ratio = lax.reduce_precision(ratio, 5, 10).astype(jnp.float16)
    step = TOP / scale_of(ratio, exponent)
    code = jnp.minimum(jnp.abs(x) * step + 0.5, TOP).astype(jnp.int32)
    power = lax.shift_left(jnp.int32(1), lax.shift_right_logical(code, 10)).astype(jnp.float32)
    size = (jnp.bitwise_and(code, 1023) + 1024).astype(jnp.float32) * power * 2.0**-24
    coded = jnp.where(x < 0, -size, size).astype(jnp.float16)
    width = x.shape[1]
    tail = jnp.concatenate(
        [jnp.broadcast_to(ratio, (TILE // 2, width)), jnp.broadcast_to(exponent, (TILE // 2, width))], 0
    )
    return jnp.concatenate([coded, tail], 0)


def decode(message):
    rows = message.shape[0] - TILE
    y = message[:rows].astype(jnp.float32)
    size = jnp.abs(y) * 2.0**14
    order = 31 - lax.clz(size.astype(jnp.int32))
    inverse = lax.shift_left(jnp.int32(1), 30 - order).astype(jnp.float32) * 2.0**-30
    code = 1024.0 * (order.astype(jnp.float32) + (size * inverse - 1.0))
    step = scale_of(message[rows : rows + 1], message[rows + TILE // 2 : rows + TILE // 2 + 1]) * (1.0 / TOP)
    return jnp.where(y < 0, -code, code) * step


def solution(mesh):
    n_row, n_col = mesh.shape["row"], mesh.shape["col"]
    q = n_row // n_col
    highest = lax.Precision.HIGHEST

    def member(x, s):
        return lax.ppermute(x, "row", [(r, r ^ s) for r in range(n_row)])

    def group(x, s):
        return lax.ppermute(x, "row", [(r, r ^ (s * q)) for r in range(n_row)])

    def plane(x, s):
        return lax.ppermute(x, "col", [(c, c ^ s) for c in range(n_col)])

    def dot(a, b, dims):
        return lax.dot_general(a, b, (dims, ((), ())), precision=highest, preferred_element_type=jnp.float32)

    def placed(pieces, me):
        rows = pieces[0].shape[0]
        whole = jnp.zeros((len(pieces) * rows, pieces[0].shape[1]), pieces[0].dtype)
        for s, piece in enumerate(pieces):
            whole = lax.dynamic_update_slice_in_dim(whole, piece, (me ^ s) * rows, 0)
        return whole

    def shards(covariance, reflectors, factor):
        rows = covariance.shape[0]
        row, c = lax.axis_index("row"), lax.axis_index("col")
        k, h = lax.div(row, q), lax.rem(row, q)
        back = lax.dot_general(
            covariance, reflectors, (((0,), (0,)), ((), ())), preferred_element_type=jnp.float32
        )
        piece = lax.dynamic_slice_in_dim(back, h * rows, rows, 0)
        for s in range(1, q):
            piece = piece + member(lax.dynamic_slice_in_dim(back, (h ^ s) * rows, rows, 0), s)
        message = encode(piece)
        others = [group(message, s) for s in range(1, n_col)]
        pieces, _ = lax.optimization_barrier((reflectors, message))
        pieces = jnp.concatenate([pieces, group(pieces, 1)], 0)
        total = piece
        for other in others:
            total = total + decode(other)
        message = encode(total)
        step = 2
        while step < n_col:
            held, _ = lax.optimization_barrier((pieces, message))
            pieces = jnp.concatenate([pieces, group(held, step)], 0)
            step *= 2
        v_mates = placed(jnp.split(pieces, n_col, 0), k)
        mates = [plane(message, s) for s in range(1, n_col)]
        held, _ = lax.optimization_barrier((total, mates[0]))
        p_cols = placed([total] + [member(held, s) for s in range(1, q)], h)
        p_mates = placed([total] + [decode(mate) for mate in mates], c)
        v_piece = lax.dynamic_slice_in_dim(v_mates, c * rows, rows, 0)
        v_cols = placed([v_piece] + [member(v_piece, s) for s in range(1, q)], h)
        gram = dot(v_mates.astype(jnp.float32), p_mates, ((0,), (0,)))
        whole = gram
        for s in range(1, q):
            whole = whole + member(gram, s)
        p_rows = lax.dynamic_slice_in_dim(p_mates, k * rows, rows, 0)
        y_rows = dot(reflectors.astype(jnp.float32), factor, ((1,), (1,)))
        y_cols = dot(v_cols.astype(jnp.float32), factor, ((1,), (1,)))
        first = covariance.astype(jnp.float32) - dot(y_rows, p_cols, ((1,), (1,)))
        x_rows = p_rows - dot(y_rows, whole, ((1,), (0,)))
        return first - dot(x_rows, y_cols, ((1,), (1,)))

    in_specs = (P("row", "col"), P("row", None), P())
    return jax.shard_map(shards, mesh=mesh, in_specs=in_specs, out_specs=P("row", "col"), check_vma=False)
```

```python
import functools

import jax
import jax.numpy as jnp
from jax import lax
from jax.experimental import pallas as pl
from jax.experimental.pallas import tpu as pltpu
from jax.sharding import PartitionSpec as P

TOP = 30719.0
LEAST = -100.0
TILE = 8
CHUNKS = 4


def scale_of(ratio, exponent):
    return ratio.astype(jnp.float32) * jnp.exp2(exponent.astype(jnp.float32))


def encode(x):
    top = jnp.max(jnp.abs(x), axis=0, keepdims=True)
    exponent = lax.reduce_precision(jnp.maximum(jnp.ceil(jnp.log2(top)), LEAST), 5, 10).astype(jnp.float16)
    ratio = jnp.clip(top * jnp.exp2(-exponent.astype(jnp.float32)) * 1.001, 0.25, 2.0)
    ratio = lax.reduce_precision(ratio, 5, 10).astype(jnp.float16)
    step = TOP / scale_of(ratio, exponent)
    code = jnp.minimum(jnp.abs(x) * step + 0.5, TOP).astype(jnp.int32)
    power = lax.shift_left(jnp.int32(1), lax.shift_right_logical(code, 10)).astype(jnp.float32)
    size = (jnp.bitwise_and(code, 1023) + 1024).astype(jnp.float32) * power * 2.0**-24
    coded = jnp.where(x < 0, -size, size).astype(jnp.float16)
    width = x.shape[1]
    tail = jnp.concatenate(
        [jnp.broadcast_to(ratio, (TILE // 2, width)), jnp.broadcast_to(exponent, (TILE // 2, width))], 0
    )
    return jnp.concatenate([coded, tail], 0)


def decode(message):
    rows = message.shape[0] - TILE
    y = message[:rows].astype(jnp.float32)
    size = jnp.abs(y) * 2.0**14
    order = 31 - lax.clz(size.astype(jnp.int32))
    inverse = lax.shift_left(jnp.int32(1), 30 - order).astype(jnp.float32) * 2.0**-30
    code = 1024.0 * (order.astype(jnp.float32) + (size * inverse - 1.0))
    step = scale_of(message[rows : rows + 1], message[rows + TILE // 2 : rows + TILE // 2 + 1]) * (1.0 / TOP)
    return jnp.where(y < 0, -code, code) * step


def halves(x):
    high = x.astype(jnp.bfloat16)
    return high, (x - high.astype(jnp.float32)).astype(jnp.bfloat16)


def dot3(a, b):
    ah, al = halves(a)
    bh, bl = halves(b)
    left = jnp.concatenate([ah, ah, al], 1)
    right = jnp.concatenate([bh, bl, bh], 0)
    return jnp.dot(left, right, preferred_element_type=jnp.float32)


def finish(q, h_ref, a_ref, v_ref, y_ref, t_ref, p_ref, w_ref, piece_ref, g_ref, *rest):
    others, (out_ref, left, right, held, sems) = rest[: q - 1], rest[q - 1 :]
    rows, band = p_ref.shape
    h = h_ref[0]
    gram = g_ref[...]
    for other in others:
        gram = gram + other[pl.ds(0, band), :]
    wide = dot3(p_ref[...] - dot3(y_ref[...], gram), t_ref[...])
    high, low = halves(wide)
    left[...] = jnp.concatenate([v_ref[...], v_ref[...], high, low], 1)
    high, low = halves(w_ref[...])
    right[:, 0:band] = high
    right[:, band : 2 * band] = low
    for s in range(q):
        v = piece_ref[...] if s == 0 else others[s - 1][pl.ds(band, rows), :].astype(jnp.bfloat16)
        at = pl.ds(pl.multiple_of((h ^ s) * rows, rows), rows)
        right[at, 2 * band : 3 * band] = v
        right[at, 3 * band : 4 * band] = v
    part = rows // CHUNKS
    copies = []
    for i in range(CHUNKS):
        at = pl.ds(i * part, part)
        product = lax.dot_general(
            left[at, :], right[...], (((1,), (1,)), ((), ())), preferred_element_type=jnp.float32
        )
        held[at, :] = a_ref[at, :].astype(jnp.float32) - product
        copy = pltpu.make_async_copy(held.at[at, :], out_ref.at[at, :], sems.at[i])
        copy.start()
        copies.append(copy)
    for copy in copies:
        copy.wait()


def solution(mesh):
    n_row, n_col = mesh.shape["row"], mesh.shape["col"]
    q = n_row // n_col
    highest = lax.Precision.HIGHEST

    def member(x, s):
        return lax.ppermute(x, "row", [(r, r ^ s) for r in range(n_row)])

    def group(x, s):
        return lax.ppermute(x, "row", [(r, r ^ (s * q)) for r in range(n_row)])

    def plane(x, s):
        return lax.ppermute(x, "col", [(c, c ^ s) for c in range(n_col)])

    def dot(a, b, dims):
        return lax.dot_general(a, b, (dims, ((), ())), precision=highest, preferred_element_type=jnp.float32)

    def placed(pieces, me):
        rows = pieces[0].shape[0]
        whole = jnp.zeros((len(pieces) * rows, pieces[0].shape[1]), pieces[0].dtype)
        for s, piece in enumerate(pieces):
            whole = lax.dynamic_update_slice_in_dim(whole, piece, (me ^ s) * rows, 0)
        return whole

    def shards(covariance, reflectors, factor):
        rows, cols = covariance.shape
        band = reflectors.shape[1]
        row, c = lax.axis_index("row"), lax.axis_index("col")
        k, h = lax.div(row, q), lax.rem(row, q)
        back = lax.dot_general(
            covariance, reflectors, (((0,), (0,)), ((), ())), preferred_element_type=jnp.float32
        )
        piece = lax.dynamic_slice_in_dim(back, h * rows, rows, 0)
        y_rows = dot(reflectors.astype(jnp.float32), factor, ((1,), (1,)))
        for s in range(1, q):
            other = member(lax.dynamic_slice_in_dim(back, (h ^ s) * rows, rows, 0), s)
            other, y_rows = lax.optimization_barrier((other, y_rows))
            piece = piece + other
        message = encode(piece)
        others = [group(message, s) for s in range(1, n_col)]
        pieces, _ = lax.optimization_barrier((reflectors, message))
        pieces = jnp.concatenate([pieces, group(pieces, 1)], 0)
        total = piece
        for other in others:
            total = total + decode(other)
        message = encode(total)
        step = 2
        while step < n_col:
            held, _ = lax.optimization_barrier((pieces, message))
            pieces = jnp.concatenate([pieces, group(held, step)], 0)
            step *= 2
        order = sorted(range(1, n_col), key=lambda s: (s < n_col // 2, s))
        mates = {s: plane(message, s) for s in order}
        held, _ = lax.optimization_barrier((total, mates[order[0]]))
        p_cols = placed([total] + [member(held, s) for s in range(1, q)], h)
        w_cols = dot(p_cols, factor, ((1,), (0,)))
        values = {0: total}
        for s in order[:-1]:
            values[s] = decode(mates[s])
        last, pieces, w_cols, values = lax.optimization_barrier((mates[order[-1]], pieces, w_cols, values))
        values[order[-1]] = decode(last)
        v_mates = placed(jnp.split(pieces, n_col, 0), k)

        def v_tile(index):
            return lax.dynamic_slice_in_dim(v_mates, index * rows, rows, 0)

        p_rows = total
        for s in order:
            p_rows = jnp.where((k ^ c) == s, values[s], p_rows)
        p_mates = placed([values[s] for s in range(n_col)], c)
        gram = dot(v_mates.astype(jnp.float32), p_mates, ((0,), (0,)))
        v_piece = v_tile(c)
        packed = jnp.concatenate([gram, v_piece.astype(jnp.float32)], 0)
        received = [member(packed, s) for s in range(1, q)]
        size = 4 * rows * cols + 2 * rows * cols + 16 * band * (rows + 2 * cols) + (q + 4) * 8 * rows * band
        vmem = pl.BlockSpec(memory_space=pltpu.VMEM)
        return pl.pallas_call(
            functools.partial(finish, q),
            out_shape=jax.ShapeDtypeStruct((rows, cols), jnp.float32),
            in_specs=[pl.BlockSpec(memory_space=pltpu.SMEM)] + [vmem] * (7 + q),
            out_specs=pl.BlockSpec(memory_space=pl.ANY),
            scratch_shapes=[
                pltpu.VMEM((rows, 4 * band), jnp.bfloat16),
                pltpu.VMEM((cols, 4 * band), jnp.bfloat16),
                pltpu.VMEM((rows, cols), jnp.float32),
                pltpu.SemaphoreType.DMA((CHUNKS,)),
            ],
            compiler_params=pltpu.CompilerParams(vmem_limit_bytes=size + (8 << 20)),
            cost_estimate=pl.CostEstimate(
                flops=2 * rows * cols * 4 * band, bytes_accessed=6 * rows * cols, transcendentals=0
            ),
        )(jnp.full((1,), h, jnp.int32), covariance, reflectors, y_rows, factor, p_rows, w_cols, v_piece, gram, *received)

    in_specs = (P("row", "col"), P("row", None), P())
    return jax.shard_map(shards, mesh=mesh, in_specs=in_specs, out_specs=P("row", "col"), check_vma=False)
```

```python
import functools

import jax
import jax.numpy as jnp
from jax import lax
from jax.experimental import pallas as pl
from jax.experimental.pallas import tpu as pltpu
from jax.sharding import PartitionSpec as P

TOP = 30719.0
LEAST = -100.0
TILE = 8
CHUNKS = 2


def scale_of(ratio, exponent):
    return ratio.astype(jnp.float32) * jnp.exp2(exponent.astype(jnp.float32))


def encode(x, top):
    exponent = lax.reduce_precision(jnp.maximum(jnp.ceil(jnp.log2(top)), LEAST), 5, 10).astype(jnp.float16)
    ratio = jnp.clip(top * jnp.exp2(-exponent.astype(jnp.float32)) * 1.001, 0.25, 2.0)
    ratio = lax.reduce_precision(ratio, 5, 10).astype(jnp.float16)
    step = TOP / scale_of(ratio, exponent)
    code = jnp.minimum(jnp.abs(x) * step + 0.5, TOP).astype(jnp.int32)
    power = lax.shift_left(jnp.int32(1), lax.shift_right_logical(code, 10)).astype(jnp.float32)
    size = (jnp.bitwise_and(code, 1023) + 1024).astype(jnp.float32) * power * 2.0**-24
    coded = jnp.where(x < 0, -size, size).astype(jnp.float16)
    width = x.shape[1]
    tail = jnp.concatenate(
        [jnp.broadcast_to(ratio, (TILE // 2, width)), jnp.broadcast_to(exponent, (TILE // 2, width))], 0
    )
    return jnp.concatenate([coded, tail], 0)


def scale_in(message):
    rows = message.shape[0] - TILE
    return scale_of(message[rows : rows + 1], message[rows + TILE // 2 : rows + TILE // 2 + 1])


def decode(message):
    rows = message.shape[0] - TILE
    y = message[:rows].astype(jnp.float32)
    size = jnp.abs(y) * 2.0**14
    order = 31 - lax.clz(size.astype(jnp.int32))
    inverse = lax.shift_left(jnp.int32(1), 30 - order).astype(jnp.float32) * 2.0**-30
    code = 1024.0 * (order.astype(jnp.float32) + (size * inverse - 1.0))
    step = scale_in(message) * (1.0 / TOP)
    return jnp.where(y < 0, -code, code) * step


def halves(x):
    high = x.astype(jnp.bfloat16)
    return high, (x - high.astype(jnp.float32)).astype(jnp.bfloat16)


def dot3(a, b):
    ah, al = halves(a)
    bh, bl = halves(b)
    left = jnp.concatenate([ah, ah, al], 1)
    right = jnp.concatenate([bh, bl, bh], 0)
    return jnp.dot(left, right, preferred_element_type=jnp.float32)


def finish(q, h_ref, a_ref, v_ref, y_ref, t_ref, p_ref, w_ref, piece_ref, g_ref, *rest):
    others, (out_ref, left, right, held, sems) = rest[: q - 1], rest[q - 1 :]
    rows, band = p_ref.shape
    h = h_ref[0]
    gram = g_ref[...]
    for other in others:
        gram = gram + other[pl.ds(0, band), :]
    wide = dot3(p_ref[...] - dot3(y_ref[...], gram), t_ref[...])
    high, low = halves(wide)
    left[...] = jnp.concatenate([v_ref[...], v_ref[...], high, low], 1)
    high, low = halves(w_ref[...])
    right[:, 0:band] = high
    right[:, band : 2 * band] = low
    for s in range(q):
        v = piece_ref[...] if s == 0 else others[s - 1][pl.ds(band, rows), :].astype(jnp.bfloat16)
        at = pl.ds(pl.multiple_of((h ^ s) * rows, rows), rows)
        right[at, 2 * band : 3 * band] = v
        right[at, 3 * band : 4 * band] = v
    part = a_ref.shape[1] // CHUNKS
    copies = []
    for i in range(CHUNKS):
        at = pl.ds(i * part, part)
        product = lax.dot_general(
            left[...], right[at, :], (((1,), (1,)), ((), ())), preferred_element_type=jnp.float32
        )
        held[:, at] = a_ref[:, at].astype(jnp.float32) - product
        copy = pltpu.make_async_copy(held.at[:, at], out_ref.at[:, at], sems.at[i])
        copy.start()
        copies.append(copy)
    for copy in copies:
        copy.wait()


def solution(mesh):
    n_row, n_col = mesh.shape["row"], mesh.shape["col"]
    q = n_row // n_col
    highest = lax.Precision.HIGHEST

    def member(x, s):
        return lax.ppermute(x, "row", [(r, r ^ s) for r in range(n_row)])

    def group(x, s):
        return lax.ppermute(x, "row", [(r, r ^ (s * q)) for r in range(n_row)])

    def plane(x, s):
        return lax.ppermute(x, "col", [(c, c ^ s) for c in range(n_col)])

    def dot(a, b, dims):
        return lax.dot_general(a, b, (dims, ((), ())), precision=highest, preferred_element_type=jnp.float32)

    def placed(pieces, me):
        rows = pieces[0].shape[0]
        whole = jnp.zeros((len(pieces) * rows, pieces[0].shape[1]), pieces[0].dtype)
        for s, piece in enumerate(pieces):
            whole = lax.dynamic_update_slice_in_dim(whole, piece, (me ^ s) * rows, 0)
        return whole

    def shards(covariance, reflectors, factor):
        rows, cols = covariance.shape
        band = reflectors.shape[1]
        row, c = lax.axis_index("row"), lax.axis_index("col")
        k, h = lax.div(row, q), lax.rem(row, q)
        y_rows = dot(reflectors.astype(jnp.float32), factor, ((1,), (1,)))

        def chip_part(tile, vectors):
            half = lax.dynamic_slice_in_dim(tile, h * rows, rows, 1)
            return lax.dot_general(half, vectors, (((0,), (0,)), ((), ())), preferred_element_type=jnp.float32)

        piece = chip_part(covariance, reflectors)
        for s in range(1, q):
            tile, vectors, piece = lax.optimization_barrier((member(covariance, s), member(reflectors, s), piece))
            piece = piece + chip_part(tile, vectors)
        message = encode(piece, jnp.max(jnp.abs(piece), axis=0, keepdims=True))
        top = scale_in(message)
        others = [group(message, s) for s in range(1, n_col)]
        pieces, _ = lax.optimization_barrier((reflectors, message))
        pieces = jnp.concatenate([pieces, group(pieces, 1)], 0)
        total, others[-1], y_rows = lax.optimization_barrier((piece, others[-1], y_rows))
        for other in others:
            total = total + decode(other)
            top = top + scale_in(other)
        message = encode(total, top)
        step = 2
        while step < n_col:
            held, _ = lax.optimization_barrier((pieces, message))
            pieces = jnp.concatenate([pieces, group(held, step)], 0)
            step *= 2
        order = sorted(range(1, n_col), key=lambda s: (s < n_col // 2, s))
        mates = {s: plane(message, s) for s in order}
        held, _ = lax.optimization_barrier((total, mates[order[0]]))
        p_cols = placed([total] + [member(held, s) for s in range(1, q)], h)
        w_cols = dot(p_cols, factor, ((1,), (0,)))
        values = {0: total}
        for s in order[:-1]:
            mate = mates[s]
            values[s] = decode(mate)
        last, pieces, values = lax.optimization_barrier((mates[order[-1]], pieces, values))
        values[order[-1]] = decode(last)
        tiles = jnp.split(pieces, n_col, 0)
        bit = 1
        while bit < n_col:
            swap = ((k ^ c) & bit) != 0
            tiles = [jnp.where(swap, tiles[s ^ bit], tiles[s]) for s in range(n_col)]
            bit *= 2
        v_mates = jnp.concatenate(tiles, 0)
        p_rows = total
        for s in order:
            p_rows = jnp.where((k ^ c) == s, values[s], p_rows)
        p_mates = jnp.concatenate([values[s] for s in range(n_col)], 0)
        gram = dot(v_mates.astype(jnp.float32), p_mates, ((0,), (0,)))
        v_piece = tiles[0]
        packed = jnp.concatenate([gram, v_piece.astype(jnp.float32)], 0)
        received = [member(packed, s) for s in range(1, q)]
        size = 4 * rows * cols + 2 * rows * cols + 16 * band * (rows + 2 * cols) + (q + 4) * 8 * rows * band
        vmem = pl.BlockSpec(memory_space=pltpu.VMEM)
        return pl.pallas_call(
            functools.partial(finish, q),
            out_shape=jax.ShapeDtypeStruct((rows, cols), jnp.float32),
            in_specs=[pl.BlockSpec(memory_space=pltpu.SMEM)] + [vmem] * (7 + q),
            out_specs=pl.BlockSpec(memory_space=pl.ANY),
            scratch_shapes=[
                pltpu.VMEM((rows, 4 * band), jnp.bfloat16),
                pltpu.VMEM((cols, 4 * band), jnp.bfloat16),
                pltpu.VMEM((rows, cols), jnp.float32),
                pltpu.SemaphoreType.DMA((CHUNKS,)),
            ],
            compiler_params=pltpu.CompilerParams(vmem_limit_bytes=size + (8 << 20)),
            cost_estimate=pl.CostEstimate(
                flops=2 * rows * cols * 4 * band, bytes_accessed=6 * rows * cols, transcendentals=0
            ),
        )(jnp.full((1,), h, jnp.int32), covariance, reflectors, y_rows, factor, p_rows, w_cols, v_piece, gram, *received)

    in_specs = (P("row", "col"), P("row", None), P())
    return jax.shard_map(shards, mesh=mesh, in_specs=in_specs, out_specs=P("row", "col"), check_vma=False)
```

```python
import functools

import jax
import jax.numpy as jnp
from jax import lax
from jax.experimental import pallas as pl
from jax.experimental.pallas import tpu as pltpu
from jax.sharding import PartitionSpec as P

TOP = 30719.0
LEAST = -100.0
TILE = 8
CHUNKS = 2


def scale_of(ratio, exponent):
    return ratio.astype(jnp.float32) * jnp.exp2(exponent.astype(jnp.float32))


def encode(x, top):
    exponent = lax.reduce_precision(jnp.maximum(jnp.ceil(jnp.log2(top)), LEAST), 5, 10).astype(jnp.float16)
    ratio = jnp.clip(top * jnp.exp2(-exponent.astype(jnp.float32)) * 1.001, 0.25, 2.0)
    ratio = lax.reduce_precision(ratio, 5, 10).astype(jnp.float16)
    step = TOP / scale_of(ratio, exponent)
    code = jnp.minimum(jnp.abs(x) * step + 0.5, TOP).astype(jnp.int32)
    power = lax.shift_left(jnp.int32(1), lax.shift_right_logical(code, 10)).astype(jnp.float32)
    size = (jnp.bitwise_and(code, 1023) + 1024).astype(jnp.float32) * power * 2.0**-24
    coded = jnp.where(x < 0, -size, size).astype(jnp.float16)
    width = x.shape[1]
    tail = jnp.concatenate(
        [jnp.broadcast_to(ratio, (TILE // 2, width)), jnp.broadcast_to(exponent, (TILE // 2, width))], 0
    )
    return jnp.concatenate([coded, tail], 0)


def scale_in(message):
    rows = message.shape[0] - TILE
    return scale_of(message[rows : rows + 1], message[rows + TILE // 2 : rows + TILE // 2 + 1])


def decode(message):
    rows = message.shape[0] - TILE
    y = message[:rows].astype(jnp.float32)
    size = jnp.abs(y) * 2.0**14
    order = 31 - lax.clz(size.astype(jnp.int32))
    inverse = lax.shift_left(jnp.int32(1), 30 - order).astype(jnp.float32) * 2.0**-30
    code = 1024.0 * (order.astype(jnp.float32) + (size * inverse - 1.0))
    step = scale_in(message) * (1.0 / TOP)
    return jnp.where(y < 0, -code, code) * step


def halves(x):
    high = x.astype(jnp.bfloat16)
    return high, (x - high.astype(jnp.float32)).astype(jnp.bfloat16)


def dot3(a, b):
    ah, al = halves(a)
    bh, bl = halves(b)
    left = jnp.concatenate([ah, ah, al], 1)
    right = jnp.concatenate([bh, bl, bh], 0)
    return jnp.dot(left, right, preferred_element_type=jnp.float32)


def finish(q, h_ref, a_ref, v_ref, y_ref, t_ref, p_ref, w_ref, piece_ref, g_ref, *rest):
    others, (out_ref, left, right, held, sems) = rest[: q - 1], rest[q - 1 :]
    rows, band = p_ref.shape
    h = h_ref[0]
    gram = g_ref[...]
    for other in others:
        gram = gram + other[pl.ds(0, band), :].astype(jnp.float32) + other[pl.ds(band, band), :].astype(jnp.float32)
    wide = dot3(p_ref[...] - dot3(y_ref[...], gram), t_ref[...])
    high, low = halves(wide)
    left[...] = jnp.concatenate([v_ref[...], v_ref[...], high, low], 1)
    high, low = halves(w_ref[...])
    right[:, 0:band] = high
    right[:, band : 2 * band] = low
    for s in range(q):
        v = piece_ref[...] if s == 0 else others[s - 1][pl.ds(2 * band, rows), :]
        at = pl.ds(pl.multiple_of((h ^ s) * rows, rows), rows)
        right[at, 2 * band : 3 * band] = v
        right[at, 3 * band : 4 * band] = v
    part = a_ref.shape[1] // CHUNKS
    copies = []
    for i in range(CHUNKS):
        at = pl.ds(i * part, part)
        product = lax.dot_general(
            left[...], right[at, :], (((1,), (1,)), ((), ())), preferred_element_type=jnp.float32
        )
        held[:, at] = a_ref[:, at].astype(jnp.float32) - product
        copy = pltpu.make_async_copy(held.at[:, at], out_ref.at[:, at], sems.at[i])
        copy.start()
        copies.append(copy)
    for copy in copies:
        copy.wait()


def solution(mesh):
    n_row, n_col = mesh.shape["row"], mesh.shape["col"]
    q = n_row // n_col
    highest = lax.Precision.HIGHEST

    def member(x, s):
        return lax.ppermute(x, "row", [(r, r ^ s) for r in range(n_row)])

    def group(x, s):
        return lax.ppermute(x, "row", [(r, r ^ (s * q)) for r in range(n_row)])

    def plane(x, s):
        return lax.ppermute(x, "col", [(c, c ^ s) for c in range(n_col)])

    def dot(a, b, dims):
        return lax.dot_general(a, b, (dims, ((), ())), precision=highest, preferred_element_type=jnp.float32)

    def placed(pieces, me):
        rows = pieces[0].shape[0]
        whole = jnp.zeros((len(pieces) * rows, pieces[0].shape[1]), pieces[0].dtype)
        for s, piece in enumerate(pieces):
            whole = lax.dynamic_update_slice_in_dim(whole, piece, (me ^ s) * rows, 0)
        return whole

    def shards(covariance, reflectors, factor):
        rows, cols = covariance.shape
        band = reflectors.shape[1]
        row, c = lax.axis_index("row"), lax.axis_index("col")
        k, h = lax.div(row, q), lax.rem(row, q)
        y_rows = dot(reflectors.astype(jnp.float32), factor, ((1,), (1,)))

        def chip_part(tile, vectors):
            half = lax.dynamic_slice_in_dim(tile, h * rows, rows, 1)
            return lax.dot_general(half, vectors, (((0,), (0,)), ((), ())), preferred_element_type=jnp.float32)

        piece = chip_part(covariance, reflectors)
        for s in range(1, q):
            tile, vectors, piece = lax.optimization_barrier((member(covariance, s), member(reflectors, s), piece))
            piece = piece + chip_part(tile, vectors)
        message = encode(piece, jnp.max(jnp.abs(piece), axis=0, keepdims=True))
        top = scale_in(message)
        others = [group(message, s) for s in range(1, n_col)]
        pieces, _ = lax.optimization_barrier((reflectors, message))
        pieces = jnp.concatenate([pieces, group(pieces, 1)], 0)
        total, others[-1], y_rows = lax.optimization_barrier((piece, others[-1], y_rows))
        for other in others:
            total = total + decode(other)
            top = top + scale_in(other)
        message = encode(total, top)
        step = 2
        while step < n_col:
            held, _ = lax.optimization_barrier((pieces, message))
            pieces = jnp.concatenate([pieces, group(held, step)], 0)
            step *= 2
        order = sorted(range(1, n_col), key=lambda s: (s < n_col // 2, s))
        mates = {s: plane(message, s) for s in order}
        held, _ = lax.optimization_barrier((total, mates[order[0]]))
        p_cols = placed([total] + [member(held, s) for s in range(1, q)], h)
        w_cols = dot(p_cols, factor, ((1,), (0,)))
        values = {0: total}
        for s in order[:-1]:
            mate = mates[s]
            values[s] = decode(mate)
        last, pieces, values = lax.optimization_barrier((mates[order[-1]], pieces, values))
        values[order[-1]] = decode(last)
        tiles = jnp.split(pieces, n_col, 0)
        bit = 1
        while bit < n_col:
            swap = ((k ^ c) & bit) != 0
            tiles = [jnp.where(swap, tiles[s ^ bit], tiles[s]) for s in range(n_col)]
            bit *= 2
        v_mates = jnp.concatenate(tiles, 0)
        p_rows = total
        for s in order:
            p_rows = jnp.where((k ^ c) == s, values[s], p_rows)
        p_mates = jnp.concatenate([values[s] for s in range(n_col)], 0)
        gram = dot(v_mates.astype(jnp.float32), p_mates, ((0,), (0,)))
        v_piece = tiles[0]
        high = lax.reduce_precision(gram, 8, 7)
        packed = jnp.concatenate([high.astype(jnp.bfloat16), (gram - high).astype(jnp.bfloat16), v_piece], 0)
        received = [member(packed, s) for s in range(1, q)]
        size = 4 * rows * cols + 2 * rows * cols + 16 * band * (rows + 2 * cols) + (q + 4) * 8 * rows * band
        vmem = pl.BlockSpec(memory_space=pltpu.VMEM)
        return pl.pallas_call(
            functools.partial(finish, q),
            out_shape=jax.ShapeDtypeStruct((rows, cols), jnp.float32),
            in_specs=[pl.BlockSpec(memory_space=pltpu.SMEM)] + [vmem] * (7 + q),
            out_specs=pl.BlockSpec(memory_space=pl.ANY),
            scratch_shapes=[
                pltpu.VMEM((rows, 4 * band), jnp.bfloat16),
                pltpu.VMEM((cols, 4 * band), jnp.bfloat16),
                pltpu.VMEM((rows, cols), jnp.float32),
                pltpu.SemaphoreType.DMA((CHUNKS,)),
            ],
            compiler_params=pltpu.CompilerParams(vmem_limit_bytes=size + (8 << 20)),
            cost_estimate=pl.CostEstimate(
                flops=2 * rows * cols * 4 * band, bytes_accessed=6 * rows * cols, transcendentals=0
            ),
        )(jnp.full((1,), h, jnp.int32), covariance, reflectors, y_rows, factor, p_rows, w_cols, v_piece, gram, *received)

    in_specs = (P("row", "col"), P("row", None), P())
    return jax.shard_map(shards, mesh=mesh, in_specs=in_specs, out_specs=P("row", "col"), check_vma=False)
```

```python
import functools
import itertools

import jax
import jax.numpy as jnp
from jax import lax
from jax.experimental import pallas as pl
from jax.experimental.pallas import tpu as pltpu
from jax.sharding import PartitionSpec as P

TOP = 30719.0
LEAST = -100.0
TILE = 8
CHUNKS = 2
SOURCES = (
    (((0, 3), (3, 2), (0, 0), (0, 1)), ((1, 1), (1, 2), (1, 3), (0, 2)), ((2, 2), (3, 0), (2, 0), (3, 1)), ((3, 3), (2, 3), (1, 0), (2, 1))),
    (((0, 2), (1, 0), (0, 3), (1, 2)), ((1, 3), (0, 0), (0, 1), (1, 1)), ((2, 3), (3, 3), (3, 1), (2, 2)), ((3, 2), (2, 0), (2, 1), (3, 0))),
    (((0, 1), (0, 3), (1, 1), (0, 0)), ((1, 2), (1, 3), (3, 0), (1, 0)), ((3, 1), (0, 2), (2, 3), (2, 0)), ((2, 1), (2, 2), (3, 3), (3, 2))),
)


def scale_of(ratio, exponent):
    return ratio.astype(jnp.float32) * jnp.exp2(exponent.astype(jnp.float32))


def encode(x, top):
    exponent = lax.reduce_precision(jnp.maximum(jnp.ceil(jnp.log2(top)), LEAST), 5, 10).astype(jnp.float16)
    ratio = jnp.clip(top * jnp.exp2(-exponent.astype(jnp.float32)) * 1.001, 0.25, 2.0)
    ratio = lax.reduce_precision(ratio, 5, 10).astype(jnp.float16)
    step = TOP / scale_of(ratio, exponent)
    code = jnp.minimum(jnp.abs(x) * step + 0.5, TOP).astype(jnp.int32)
    power = lax.shift_left(jnp.int32(1), lax.shift_right_logical(code, 10)).astype(jnp.float32)
    size = (jnp.bitwise_and(code, 1023) + 1024).astype(jnp.float32) * power * 2.0**-24
    coded = jnp.where(x < 0, -size, size).astype(jnp.float16)
    width = x.shape[1]
    tail = jnp.concatenate(
        [jnp.broadcast_to(ratio, (TILE // 2, width)), jnp.broadcast_to(exponent, (TILE // 2, width))], 0
    )
    return jnp.concatenate([coded, tail], 0)


def scale_in(message):
    rows = message.shape[0] - TILE
    return scale_of(message[rows : rows + 1], message[rows + TILE // 2 : rows + TILE // 2 + 1])


def decode(message):
    rows = message.shape[0] - TILE
    y = message[:rows].astype(jnp.float32)
    size = jnp.abs(y) * 2.0**14
    order = 31 - lax.clz(size.astype(jnp.int32))
    inverse = lax.shift_left(jnp.int32(1), 30 - order).astype(jnp.float32) * 2.0**-30
    code = 1024.0 * (order.astype(jnp.float32) + (size * inverse - 1.0))
    step = scale_in(message) * (1.0 / TOP)
    return jnp.where(y < 0, -code, code) * step


def halves(x):
    high = x.astype(jnp.bfloat16)
    return high, (x - high.astype(jnp.float32)).astype(jnp.bfloat16)


def dot3(a, b):
    ah, al = halves(a)
    bh, bl = halves(b)
    left = jnp.concatenate([ah, ah, al], 1)
    right = jnp.concatenate([bh, bl, bh], 0)
    return jnp.dot(left, right, preferred_element_type=jnp.float32)


def finish(q, h_ref, a_ref, v_ref, y_ref, t_ref, p_ref, w_ref, piece_ref, g_ref, *rest):
    others, (out_ref, left, right, held, sems) = rest[: q - 1], rest[q - 1 :]
    rows, band = p_ref.shape
    h = h_ref[0]
    gram = g_ref[...]
    for other in others:
        gram = gram + other[pl.ds(0, band), :].astype(jnp.float32) + other[pl.ds(band, band), :].astype(jnp.float32)
    wide = dot3(p_ref[...] - dot3(y_ref[...], gram), t_ref[...])
    high, low = halves(wide)
    left[...] = jnp.concatenate([v_ref[...], v_ref[...], high, low], 1)
    high, low = halves(w_ref[...])
    right[:, 0:band] = high
    right[:, band : 2 * band] = low
    for s in range(q):
        v = piece_ref[...] if s == 0 else others[s - 1][pl.ds(2 * band, rows), :]
        at = pl.ds(pl.multiple_of((h ^ s) * rows, rows), rows)
        right[at, 2 * band : 3 * band] = v
        right[at, 3 * band : 4 * band] = v
    part = a_ref.shape[1] // CHUNKS
    copies = []
    for i in range(CHUNKS):
        at = pl.ds(i * part, part)
        product = lax.dot_general(
            left[...], right[at, :], (((1,), (1,)), ((), ())), preferred_element_type=jnp.float32
        )
        held[:, at] = a_ref[:, at].astype(jnp.float32) - product
        copy = pltpu.make_async_copy(held.at[:, at], out_ref.at[:, at], sems.at[i])
        copy.start()
        copies.append(copy)
    for copy in copies:
        copy.wait()


def solution(mesh):
    n_row, n_col = mesh.shape["row"], mesh.shape["col"]
    q = n_row // n_col
    paired = q == 2 and n_col == 4
    highest = lax.Precision.HIGHEST

    def member(x, s):
        return lax.ppermute(x, "row", [(r, r ^ s) for r in range(n_row)])

    def group(x, s):
        return lax.ppermute(x, "row", [(r, r ^ (s * q)) for r in range(n_row)])

    def source(s, k, c):
        return SOURCES[s - 1][k][c] if n_col == len(SOURCES) + 1 else (k, c ^ s)

    def plane(x, s):
        pairs = []
        for k, h, c in itertools.product(range(n_col), range(q), range(n_col)):
            j, d = source(s, k, c)
            pairs.append(((j * q + h) * n_col + d, (k * q + h) * n_col + c))
        return lax.ppermute(x, ("row", "col"), pairs)

    def origin(s, k, c):
        bits = n_col.bit_length()
        word = jnp.int32(0)
        for i in range(n_col):
            code = sum(source(s, i, j)[1] << (bits * j) for j in range(n_col))
            word = jnp.where(k == i, jnp.int32(code), word)
        return jnp.bitwise_and(lax.shift_right_logical(word, bits * c), (1 << bits) - 1)


    def dot(a, b, dims):
        return lax.dot_general(a, b, (dims, ((), ())), precision=highest, preferred_element_type=jnp.float32)

    def by_index(pieces, me):
        return [jnp.where(me == 0, pieces[s], pieces[1 - s]) for s in range(2)]

    def placed(pieces, me):
        rows = pieces[0].shape[0]
        whole = jnp.zeros((len(pieces) * rows, pieces[0].shape[1]), pieces[0].dtype)
        for s, piece in enumerate(pieces):
            whole = lax.dynamic_update_slice_in_dim(whole, piece, (me ^ s) * rows, 0)
        return whole

    def shards(covariance, reflectors, factor):
        rows, cols = covariance.shape
        band = reflectors.shape[1]
        row, c = lax.axis_index("row"), lax.axis_index("col")
        k, h = lax.div(row, q), lax.rem(row, q)
        came = [c] + [origin(s, k, c) for s in range(1, n_col)]

        def chip_part(tile, vectors):
            half = lax.dynamic_slice_in_dim(tile, h * rows, rows, 1)
            return lax.dot_general(half, vectors, (((0,), (0,)), ((), ())), preferred_element_type=jnp.float32)

        piece = chip_part(covariance, reflectors)
        for s in range(1, q):
            tile, vectors, piece = lax.optimization_barrier((member(covariance, s), member(reflectors, s), piece))
            piece = piece + chip_part(tile, vectors)
        message = encode(piece, jnp.max(jnp.abs(piece), axis=0, keepdims=True))
        top = scale_in(message)
        others = [group(message, s) for s in reversed(range(1, n_col))]
        held, _ = lax.optimization_barrier((reflectors, message))
        y_rows = dot(held.astype(jnp.float32), factor, ((1,), (1,)))
        held, _ = lax.optimization_barrier((reflectors, message))
        if paired:
            pair, _ = lax.optimization_barrier((jnp.concatenate(by_index([reflectors, vectors], h), 0), message))
            near = lax.ppermute(
                pair, "row", [(k * q + h, (k ^ (1 << h)) * q + h) for k in range(n_col) for h in range(q)]
            )
            far = group(held, 3)
        else:
            got = [group(held, s) for s in range(1, n_col)]
        total, others[-1], y_rows = lax.optimization_barrier((piece, others[-1], y_rows))
        for other in others:
            total = total + decode(other)
            top = top + scale_in(other)
        message = encode(total, top)
        order = list(range(1, n_col))
        mates = {s: plane(message, s) for s in order}
        if paired:
            mine = lax.dynamic_slice_in_dim(near, h * rows, rows, 0)
            theirs = lax.dynamic_slice_in_dim(near, (1 - h) * rows, rows, 0)
            received = member(jnp.concatenate([total, theirs.astype(jnp.float32)], 0), 1)
            p_cols = placed([total, received[:rows]], h)
            got = by_index([mine, received[rows:].astype(jnp.bfloat16)], h) + [far]
        else:
            p_cols = placed([total] + [member(total, s) for s in range(1, q)], h)
        pieces = jnp.concatenate([reflectors] + got, 0)
        w_cols = dot(p_cols, factor, ((1,), (0,)))
        values = {0: total}
        for s in order[:-1]:
            mate = mates[s]
            values[s] = decode(mate)
        last, pieces, values = lax.optimization_barrier((mates[order[-1]], pieces, values))
        values[order[-1]] = decode(last)
        pieces = jnp.split(pieces, n_col, 0)
        tiles = []
        for s in range(n_col):
            tile = pieces[0]
            for t in range(1, n_col):
                tile = jnp.where((k ^ t) == came[s], pieces[t], tile)
            tiles.append(tile)
        v_mates = jnp.concatenate(tiles, 0)
        p_rows = total
        for s in order:
            p_rows = jnp.where(came[s] == k, values[s], p_rows)
        p_mates = jnp.concatenate([values[s] for s in range(n_col)], 0)
        gram = dot(v_mates.astype(jnp.float32), p_mates, ((0,), (0,)))
        v_piece = tiles[0]
        high = lax.reduce_precision(gram, 8, 7)
        packed = jnp.concatenate([high.astype(jnp.bfloat16), (gram - high).astype(jnp.bfloat16), v_piece], 0)
        received = [member(packed, s) for s in range(1, q)]
        size = 4 * rows * cols + 2 * rows * cols + 16 * band * (rows + 2 * cols) + (q + 4) * 8 * rows * band
        vmem = pl.BlockSpec(memory_space=pltpu.VMEM)
        return pl.pallas_call(
            functools.partial(finish, q),
            out_shape=jax.ShapeDtypeStruct((rows, cols), jnp.float32),
            in_specs=[pl.BlockSpec(memory_space=pltpu.SMEM)] + [vmem] * (7 + q),
            out_specs=pl.BlockSpec(memory_space=pl.ANY),
            scratch_shapes=[
                pltpu.VMEM((rows, 4 * band), jnp.bfloat16),
                pltpu.VMEM((cols, 4 * band), jnp.bfloat16),
                pltpu.VMEM((rows, cols), jnp.float32),
                pltpu.SemaphoreType.DMA((CHUNKS,)),
            ],
            compiler_params=pltpu.CompilerParams(vmem_limit_bytes=size + (8 << 20)),
            cost_estimate=pl.CostEstimate(
                flops=2 * rows * cols * 4 * band, bytes_accessed=6 * rows * cols, transcendentals=0
            ),
        )(jnp.full((1,), h, jnp.int32), covariance, reflectors, y_rows, factor, p_rows, w_cols, v_piece, gram, *received)

    in_specs = (P("row", "col"), P("row", None), P())
    return jax.shard_map(shards, mesh=mesh, in_specs=in_specs, out_specs=P("row", "col"), check_vma=False)
```

```python
import functools
import itertools

import jax
import jax.numpy as jnp
from jax import lax
from jax.experimental import pallas as pl
from jax.experimental.pallas import tpu as pltpu
from jax.sharding import PartitionSpec as P

TOP = 30719.0
LEAST = -100.0
TILE = 8
CHUNKS = 2
SOURCES = (
    (((0, 3), (1, 0), (0, 0), (0, 1)), ((1, 1), (3, 2), (1, 3), (0, 2)), ((2, 2), (3, 3), (2, 0), (3, 1)), ((1, 2), (2, 3), (2, 1), (3, 0))),
    (((0, 2), (3, 2), (0, 3), (1, 2)), ((1, 3), (0, 0), (0, 1), (1, 1)), ((2, 3), (3, 0), (3, 1), (2, 2)), ((3, 3), (2, 0), (1, 0), (2, 1))),
    (((0, 1), (0, 3), (1, 1), (0, 0)), ((1, 2), (1, 3), (3, 0), (1, 0)), ((3, 1), (0, 2), (2, 3), (2, 0)), ((2, 1), (2, 2), (3, 3), (3, 2))),
)


def scale_of(ratio, exponent):
    return ratio.astype(jnp.float32) * jnp.exp2(exponent.astype(jnp.float32))


def encode(x, top):
    exponent = lax.reduce_precision(jnp.maximum(jnp.ceil(jnp.log2(top)), LEAST), 5, 10).astype(jnp.float16)
    ratio = jnp.clip(top * jnp.exp2(-exponent.astype(jnp.float32)) * 1.001, 0.25, 2.0)
    ratio = lax.reduce_precision(ratio, 5, 10).astype(jnp.float16)
    step = TOP / scale_of(ratio, exponent)
    code = jnp.minimum(jnp.abs(x) * step + 0.5, TOP).astype(jnp.int32)
    power = lax.shift_left(jnp.int32(1), lax.shift_right_logical(code, 10)).astype(jnp.float32)
    size = (jnp.bitwise_and(code, 1023) + 1024).astype(jnp.float32) * power * 2.0**-24
    coded = jnp.where(x < 0, -size, size).astype(jnp.float16)
    width = x.shape[1]
    tail = jnp.concatenate(
        [jnp.broadcast_to(ratio, (TILE // 2, width)), jnp.broadcast_to(exponent, (TILE // 2, width))], 0
    )
    return jnp.concatenate([coded, tail], 0)


def scale_in(message):
    rows = message.shape[0] - TILE
    return scale_of(message[rows : rows + 1], message[rows + TILE // 2 : rows + TILE // 2 + 1])


def decode(message):
    rows = message.shape[0] - TILE
    y = message[:rows].astype(jnp.float32)
    size = jnp.abs(y) * 2.0**14
    order = 31 - lax.clz(size.astype(jnp.int32))
    inverse = lax.shift_left(jnp.int32(1), 30 - order).astype(jnp.float32) * 2.0**-30
    code = 1024.0 * (order.astype(jnp.float32) + (size * inverse - 1.0))
    step = scale_in(message) * (1.0 / TOP)
    return jnp.where(y < 0, -code, code) * step


def halves(x):
    high = x.astype(jnp.bfloat16)
    return high, (x - high.astype(jnp.float32)).astype(jnp.bfloat16)


def dot3(a, b):
    ah, al = halves(a)
    bh, bl = halves(b)
    left = jnp.concatenate([ah, ah, al], 1)
    right = jnp.concatenate([bh, bl, bh], 0)
    return jnp.dot(left, right, preferred_element_type=jnp.float32)


def finish(q, h_ref, a_ref, v_ref, y_ref, t_ref, p_ref, w_ref, piece_ref, g_ref, *rest):
    others, (out_ref, left, right, held, sems) = rest[: q - 1], rest[q - 1 :]
    rows, band = p_ref.shape
    h = h_ref[0]
    gram = g_ref[...]
    for other in others:
        gram = gram + other[pl.ds(0, band), :].astype(jnp.float32) + other[pl.ds(band, band), :].astype(jnp.float32)
    wide = dot3(p_ref[...] - dot3(y_ref[...], gram), t_ref[...])
    high, low = halves(wide)
    left[...] = jnp.concatenate([v_ref[...], v_ref[...], high, low], 1)
    high, low = halves(w_ref[...])
    right[:, 0:band] = high
    right[:, band : 2 * band] = low
    for s in range(q):
        v = piece_ref[...] if s == 0 else others[s - 1][pl.ds(2 * band, rows), :]
        at = pl.ds(pl.multiple_of((h ^ s) * rows, rows), rows)
        right[at, 2 * band : 3 * band] = v
        right[at, 3 * band : 4 * band] = v
    part = a_ref.shape[1] // CHUNKS
    copies = []
    for i in range(CHUNKS):
        at = pl.ds(i * part, part)
        product = lax.dot_general(
            left[...], right[at, :], (((1,), (1,)), ((), ())), preferred_element_type=jnp.float32
        )
        held[:, at] = a_ref[:, at].astype(jnp.float32) - product
        copy = pltpu.make_async_copy(held.at[:, at], out_ref.at[:, at], sems.at[i])
        copy.start()
        copies.append(copy)
    for copy in copies:
        copy.wait()


def solution(mesh):
    n_row, n_col = mesh.shape["row"], mesh.shape["col"]
    q = n_row // n_col
    paired = q == 2 and n_col == 4
    highest = lax.Precision.HIGHEST

    def member(x, s):
        return lax.ppermute(x, "row", [(r, r ^ s) for r in range(n_row)])

    def group(x, s):
        return lax.ppermute(x, "row", [(r, r ^ (s * q)) for r in range(n_row)])

    def source(s, k, c):
        return SOURCES[s - 1][k][c] if n_col == len(SOURCES) + 1 else (k, c ^ s)

    def plane(x, s):
        pairs = []
        for k, h, c in itertools.product(range(n_col), range(q), range(n_col)):
            j, d = source(s, k, c)
            pairs.append(((j * q + h) * n_col + d, (k * q + h) * n_col + c))
        return lax.ppermute(x, ("row", "col"), pairs)

    def origin(s, k, c):
        bits = n_col.bit_length()
        word = jnp.int32(0)
        for i in range(n_col):
            code = sum(source(s, i, j)[1] << (bits * j) for j in range(n_col))
            word = jnp.where(k == i, jnp.int32(code), word)
        return jnp.bitwise_and(lax.shift_right_logical(word, bits * c), (1 << bits) - 1)


    def dot(a, b, dims):
        return lax.dot_general(a, b, (dims, ((), ())), precision=highest, preferred_element_type=jnp.float32)

    def by_index(pieces, me):
        return [jnp.where(me == 0, pieces[s], pieces[1 - s]) for s in range(2)]

    def placed(pieces, me):
        rows = pieces[0].shape[0]
        whole = jnp.zeros((len(pieces) * rows, pieces[0].shape[1]), pieces[0].dtype)
        for s, piece in enumerate(pieces):
            whole = lax.dynamic_update_slice_in_dim(whole, piece, (me ^ s) * rows, 0)
        return whole

    def shards(covariance, reflectors, factor):
        rows, cols = covariance.shape
        band = reflectors.shape[1]
        row, c = lax.axis_index("row"), lax.axis_index("col")
        k, h = lax.div(row, q), lax.rem(row, q)
        came = [c] + [origin(s, k, c) for s in range(1, n_col)]

        def chip_part(tile, vectors):
            half = lax.dynamic_slice_in_dim(tile, h * rows, rows, 1)
            return lax.dot_general(half, vectors, (((0,), (0,)), ((), ())), preferred_element_type=jnp.float32)

        piece = chip_part(covariance, reflectors)
        for s in range(1, q):
            tile, vectors, piece = lax.optimization_barrier((member(covariance, s), member(reflectors, s), piece))
            piece = piece + chip_part(tile, vectors)
        message = encode(piece, jnp.max(jnp.abs(piece), axis=0, keepdims=True))
        top = scale_in(message)
        others = [group(message, s) for s in reversed(range(1, n_col))]
        held, _ = lax.optimization_barrier((reflectors, message))
        y_rows = dot(held.astype(jnp.float32), factor, ((1,), (1,)))
        held, _ = lax.optimization_barrier((reflectors, message))
        if paired:
            pair, _ = lax.optimization_barrier((jnp.concatenate(by_index([reflectors, vectors], h), 0), message))
            near = lax.ppermute(
                pair, "row", [(k * q + h, (k ^ (1 << h)) * q + h) for k in range(n_col) for h in range(q)]
            )
            far = group(held, 3)
        else:
            got = [group(held, s) for s in range(1, n_col)]
        total, others[-1], y_rows = lax.optimization_barrier((piece, others[-1], y_rows))
        for other in others:
            total = total + decode(other)
            top = top + scale_in(other)
        message = encode(total, top)
        order = list(range(1, n_col))
        mates = {s: plane(message, s) for s in order}
        if paired:
            mine = lax.dynamic_slice_in_dim(near, h * rows, rows, 0)
            theirs = lax.dynamic_slice_in_dim(near, (1 - h) * rows, rows, 0)
            received = member(jnp.concatenate([total, theirs.astype(jnp.float32)], 0), 1)
            p_cols = placed([total, received[:rows]], h)
            got = by_index([mine, received[rows:].astype(jnp.bfloat16)], h) + [far]
        else:
            p_cols = placed([total] + [member(total, s) for s in range(1, q)], h)
        pieces = jnp.concatenate([reflectors] + got, 0)
        w_cols = dot(p_cols, factor, ((1,), (0,)))
        values = {0: total}
        for s in order[:-1]:
            mate = mates[s]
            values[s] = decode(mate)
        last, pieces, values = lax.optimization_barrier((mates[order[-1]], pieces, values))
        values[order[-1]] = decode(last)
        pieces = jnp.split(pieces, n_col, 0)
        tiles = []
        for s in range(n_col):
            tile = pieces[0]
            for t in range(1, n_col):
                tile = jnp.where((k ^ t) == came[s], pieces[t], tile)
            tiles.append(tile)
        v_mates = jnp.concatenate(tiles, 0)
        p_rows = total
        for s in order:
            p_rows = jnp.where(came[s] == k, values[s], p_rows)
        p_mates = jnp.concatenate([values[s] for s in range(n_col)], 0)
        gram = dot(v_mates.astype(jnp.float32), p_mates, ((0,), (0,)))
        v_piece = tiles[0]
        high = lax.reduce_precision(gram, 8, 7)
        packed = jnp.concatenate([high.astype(jnp.bfloat16), (gram - high).astype(jnp.bfloat16), v_piece], 0)
        received = [member(packed, s) for s in range(1, q)]
        size = 4 * rows * cols + 2 * rows * cols + 16 * band * (rows + 2 * cols) + (q + 4) * 8 * rows * band
        vmem = pl.BlockSpec(memory_space=pltpu.VMEM)
        return pl.pallas_call(
            functools.partial(finish, q),
            out_shape=jax.ShapeDtypeStruct((rows, cols), jnp.float32),
            in_specs=[pl.BlockSpec(memory_space=pltpu.SMEM)] + [vmem] * (7 + q),
            out_specs=pl.BlockSpec(memory_space=pl.ANY),
            scratch_shapes=[
                pltpu.VMEM((rows, 4 * band), jnp.bfloat16),
                pltpu.VMEM((cols, 4 * band), jnp.bfloat16),
                pltpu.VMEM((rows, cols), jnp.float32),
                pltpu.SemaphoreType.DMA((CHUNKS,)),
            ],
            compiler_params=pltpu.CompilerParams(vmem_limit_bytes=size + (8 << 20)),
            cost_estimate=pl.CostEstimate(
                flops=2 * rows * cols * 4 * band, bytes_accessed=6 * rows * cols, transcendentals=0
            ),
        )(jnp.full((1,), h, jnp.int32), covariance, reflectors, y_rows, factor, p_rows, w_cols, v_piece, gram, *received)

    in_specs = (P("row", "col"), P("row", None), P())
    return jax.shard_map(shards, mesh=mesh, in_specs=in_specs, out_specs=P("row", "col"), check_vma=False)
```

```python
import functools
import itertools

import jax
import jax.numpy as jnp
from jax import lax
from jax.experimental import pallas as pl
from jax.experimental.pallas import tpu as pltpu
from jax.sharding import PartitionSpec as P

TOP = 30719.0
LEAST = -100.0
TILE = 8
CHUNKS = 2
SOURCES = (
    (((0, 3), (3, 2), (0, 0), (0, 1)), ((1, 1), (1, 2), (1, 3), (0, 2)), ((2, 2), (3, 0), (2, 0), (3, 1)), ((3, 3), (2, 3), (1, 0), (2, 1))),
    (((0, 2), (1, 0), (0, 3), (1, 2)), ((1, 3), (0, 0), (0, 1), (1, 1)), ((2, 3), (3, 3), (3, 1), (2, 2)), ((3, 2), (2, 0), (2, 1), (3, 0))),
    (((0, 1), (0, 3), (1, 1), (0, 0)), ((1, 2), (1, 3), (3, 0), (1, 0)), ((3, 1), (0, 2), (2, 3), (2, 0)), ((2, 1), (2, 2), (3, 3), (3, 2))),
)


def scale_of(ratio, exponent):
    return ratio.astype(jnp.float32) * jnp.exp2(exponent.astype(jnp.float32))


def encode(x, top):
    exponent = lax.reduce_precision(jnp.maximum(jnp.ceil(jnp.log2(top)), LEAST), 5, 10).astype(jnp.float16)
    ratio = jnp.clip(top * jnp.exp2(-exponent.astype(jnp.float32)) * 1.001, 0.25, 2.0)
    ratio = lax.reduce_precision(ratio, 5, 10).astype(jnp.float16)
    step = TOP / scale_of(ratio, exponent)
    code = jnp.minimum(jnp.abs(x) * step + 0.5, TOP).astype(jnp.int32)
    power = lax.shift_left(jnp.int32(1), lax.shift_right_logical(code, 10)).astype(jnp.float32)
    size = (jnp.bitwise_and(code, 1023) + 1024).astype(jnp.float32) * power * 2.0**-24
    coded = jnp.where(x < 0, -size, size).astype(jnp.float16)
    width = x.shape[1]
    tail = jnp.concatenate(
        [jnp.broadcast_to(ratio, (TILE // 2, width)), jnp.broadcast_to(exponent, (TILE // 2, width))], 0
    )
    return jnp.concatenate([coded, tail], 0)


def scale_in(message):
    rows = message.shape[0] - TILE
    return scale_of(message[rows : rows + 1], message[rows + TILE // 2 : rows + TILE // 2 + 1])


def decode(message):
    rows = message.shape[0] - TILE
    y = message[:rows].astype(jnp.float32)
    size = jnp.abs(y) * 2.0**14
    order = 31 - lax.clz(size.astype(jnp.int32))
    inverse = lax.shift_left(jnp.int32(1), 30 - order).astype(jnp.float32) * 2.0**-30
    code = 1024.0 * (order.astype(jnp.float32) + (size * inverse - 1.0))
    step = scale_in(message) * (1.0 / TOP)
    return jnp.where(y < 0, -code, code) * step


def halves(x):
    high = x.astype(jnp.bfloat16)
    return high, (x - high.astype(jnp.float32)).astype(jnp.bfloat16)


def dot3(a, b):
    ah, al = halves(a)
    bh, bl = halves(b)
    left = jnp.concatenate([ah, ah, al], 1)
    right = jnp.concatenate([bh, bl, bh], 0)
    return jnp.dot(left, right, preferred_element_type=jnp.float32)


def finish(q, h_ref, a_ref, v_ref, y_ref, t_ref, p_ref, w_ref, piece_ref, g_ref, *rest):
    others, (out_ref, left, right, held, sems) = rest[: q - 1], rest[q - 1 :]
    rows, band = p_ref.shape
    h = h_ref[0]
    gram = g_ref[...]
    for other in others:
        gram = gram + other[pl.ds(0, band), :].astype(jnp.float32) + other[pl.ds(band, band), :].astype(jnp.float32)
    wide = dot3(p_ref[...] - dot3(y_ref[...], gram), t_ref[...])
    high, low = halves(wide)
    left[...] = jnp.concatenate([v_ref[...], v_ref[...], high, low], 1)
    high, low = halves(w_ref[...])
    right[:, 0:band] = high
    right[:, band : 2 * band] = low
    for s in range(q):
        v = piece_ref[...] if s == 0 else others[s - 1][pl.ds(2 * band, rows), :]
        at = pl.ds(pl.multiple_of((h ^ s) * rows, rows), rows)
        right[at, 2 * band : 3 * band] = v
        right[at, 3 * band : 4 * band] = v
    part = a_ref.shape[1] // CHUNKS
    copies = []
    for i in range(CHUNKS):
        at = pl.ds(i * part, part)
        product = lax.dot_general(
            left[...], right[at, :], (((1,), (1,)), ((), ())), preferred_element_type=jnp.float32
        )
        held[:, at] = a_ref[:, at].astype(jnp.float32) - product
        copy = pltpu.make_async_copy(held.at[:, at], out_ref.at[:, at], sems.at[i])
        copy.start()
        copies.append(copy)
    for copy in copies:
        copy.wait()


def solution(mesh):
    n_row, n_col = mesh.shape["row"], mesh.shape["col"]
    q = n_row // n_col
    paired = q == 2 and n_col == 4
    highest = lax.Precision.HIGHEST

    def member(x, s):
        return lax.ppermute(x, "row", [(r, r ^ s) for r in range(n_row)])

    def group(x, s):
        return lax.ppermute(x, "row", [(r, r ^ (s * q)) for r in range(n_row)])

    def source(s, k, c):
        return SOURCES[s - 1][k][c] if n_col == len(SOURCES) + 1 else (k, c ^ s)

    def plane(x, s):
        pairs = []
        for k, h, c in itertools.product(range(n_col), range(q), range(n_col)):
            j, d = source(s, k, c)
            pairs.append(((j * q + h) * n_col + d, (k * q + h) * n_col + c))
        return lax.ppermute(x, ("row", "col"), pairs)

    def origin(s, k, c):
        bits = n_col.bit_length()
        word = jnp.int32(0)
        for i in range(n_col):
            code = sum(source(s, i, j)[1] << (bits * j) for j in range(n_col))
            word = jnp.where(k == i, jnp.int32(code), word)
        return jnp.bitwise_and(lax.shift_right_logical(word, bits * c), (1 << bits) - 1)


    def dot(a, b, dims):
        return lax.dot_general(a, b, (dims, ((), ())), precision=highest, preferred_element_type=jnp.float32)

    def by_index(pieces, me):
        return [jnp.where(me == 0, pieces[s], pieces[1 - s]) for s in range(2)]

    def placed(pieces, me):
        rows = pieces[0].shape[0]
        whole = jnp.zeros((len(pieces) * rows, pieces[0].shape[1]), pieces[0].dtype)
        for s, piece in enumerate(pieces):
            whole = lax.dynamic_update_slice_in_dim(whole, piece, (me ^ s) * rows, 0)
        return whole

    def shards(covariance, reflectors, factor):
        rows, cols = covariance.shape
        band = reflectors.shape[1]
        row, c = lax.axis_index("row"), lax.axis_index("col")
        k, h = lax.div(row, q), lax.rem(row, q)
        came = [c] + [origin(s, k, c) for s in range(1, n_col)]

        def chip_part(tile, vectors):
            half = lax.dynamic_slice_in_dim(tile, h * rows, rows, 1)
            return lax.dot_general(half, vectors, (((0,), (0,)), ((), ())), preferred_element_type=jnp.float32)

        piece = chip_part(covariance, reflectors)
        for s in range(1, q):
            tile, vectors, piece = lax.optimization_barrier((member(covariance, s), member(reflectors, s), piece))
            piece = piece + chip_part(tile, vectors)
        message = encode(piece, jnp.max(jnp.abs(piece), axis=0, keepdims=True))
        top = scale_in(message)
        others = [group(message, s) for s in reversed(range(1, n_col))]
        held, _ = lax.optimization_barrier((reflectors, message))
        y_rows = dot(held.astype(jnp.float32), factor, ((1,), (1,)))
        held, _ = lax.optimization_barrier((reflectors, message))
        if paired:
            pair, _ = lax.optimization_barrier((jnp.concatenate(by_index([reflectors, vectors], h), 0), message))
            near = lax.ppermute(
                pair, "row", [(k * q + h, (k ^ (1 << h)) * q + h) for k in range(n_col) for h in range(q)]
            )
            far = group(held, 3)
        else:
            got = [group(held, s) for s in range(1, n_col)]
        total, others[-1], y_rows = lax.optimization_barrier((piece, others[-1], y_rows))
        for other in others:
            total = total + decode(other)
            top = top + scale_in(other)
        message = encode(total, top)
        order = list(range(1, n_col))
        mates = {s: plane(message, s) for s in order}
        if paired:
            mine = lax.dynamic_slice_in_dim(near, h * rows, rows, 0)
            theirs = lax.dynamic_slice_in_dim(near, (1 - h) * rows, rows, 0)
            received = member(jnp.concatenate([total, theirs.astype(jnp.float32)], 0), 1)
            p_cols = placed([total, received[:rows]], h)
            got = by_index([mine, received[rows:].astype(jnp.bfloat16)], h) + [far]
        else:
            p_cols = placed([total] + [member(total, s) for s in range(1, q)], h)
        pieces = jnp.concatenate([reflectors] + got, 0)
        w_cols = dot(p_cols, factor, ((1,), (0,)))
        values = {0: total}
        for s in order[:-1]:
            mate = mates[s]
            values[s] = decode(mate)
        last, pieces, values = lax.optimization_barrier((mates[order[-1]], pieces, values))
        values[order[-1]] = decode(last)
        pieces = jnp.split(pieces, n_col, 0)
        tiles = []
        for s in range(n_col):
            tile = pieces[0]
            for t in range(1, n_col):
                tile = jnp.where((k ^ t) == came[s], pieces[t], tile)
            tiles.append(tile)
        v_mates = jnp.concatenate(tiles, 0)
        p_rows = total
        for s in order:
            p_rows = jnp.where(came[s] == k, values[s], p_rows)
        parts = [lax.reduce_precision(values[s], 8, 7) for s in range(n_col)]
        terms = [
            jnp.concatenate([parts[s].astype(jnp.bfloat16), (values[s] - parts[s]).astype(jnp.bfloat16)], 1)
            for s in range(n_col)
        ]
        gram = lax.dot_general(
            v_mates, jnp.concatenate(terms, 0), (((0,), (0,)), ((), ())), preferred_element_type=jnp.float32
        )
        gram = gram[:, :band] + gram[:, band:]
        v_piece = tiles[0]
        high = lax.reduce_precision(gram, 8, 7)
        packed = jnp.concatenate([high.astype(jnp.bfloat16), (gram - high).astype(jnp.bfloat16), v_piece], 0)
        received = [member(packed, s) for s in range(1, q)]
        size = 4 * rows * cols + 2 * rows * cols + 16 * band * (rows + 2 * cols) + (q + 4) * 8 * rows * band
        vmem = pl.BlockSpec(memory_space=pltpu.VMEM)
        return pl.pallas_call(
            functools.partial(finish, q),
            out_shape=jax.ShapeDtypeStruct((rows, cols), jnp.float32),
            in_specs=[pl.BlockSpec(memory_space=pltpu.SMEM)] + [vmem] * (7 + q),
            out_specs=pl.BlockSpec(memory_space=pl.ANY),
            scratch_shapes=[
                pltpu.VMEM((rows, 4 * band), jnp.bfloat16),
                pltpu.VMEM((cols, 4 * band), jnp.bfloat16),
                pltpu.VMEM((rows, cols), jnp.float32),
                pltpu.SemaphoreType.DMA((CHUNKS,)),
            ],
            compiler_params=pltpu.CompilerParams(vmem_limit_bytes=size + (8 << 20)),
            cost_estimate=pl.CostEstimate(
                flops=2 * rows * cols * 4 * band, bytes_accessed=6 * rows * cols, transcendentals=0
            ),
        )(jnp.full((1,), h, jnp.int32), covariance, reflectors, y_rows, factor, p_rows, w_cols, v_piece, gram, *received)

    in_specs = (P("row", "col"), P("row", None), P())
    return jax.shard_map(shards, mesh=mesh, in_specs=in_specs, out_specs=P("row", "col"), check_vma=False)
```
